256 devices in a mesh: pair: 128 (over z, y, x), col: 2 (over core).
Axes of the slice: x: 4, y: 4, z: 8, core: 2. Of those that a mesh axis runs over, the one named last changes fastest.
Arguments:
- interferograms: bfloat16 [640, 128, 1024], P('pair', None, 'col'), may hold values from -10 to 10
- coherence: bfloat16 [640, 128, 1024], P('pair', None, 'col'), may hold values from 0.099609375 to 1
- pair_epochs: int32 [640, 2], replicated, may hold values from 0 to 149, as said below
- inverse: bfloat16 [150, 640], replicated, as said below
- footprint: int32 [128, 1024], P('pair', 'col'), may hold values from 0 to 3, as said below
Outputs:
- misfit: float32 [128, 1024], P('pair', 'col')
- volumes: float32 [150, 512], P(None, ('pair', 'col'))
The draws below stay inside these ranges and needn't reach their ends.
Inputs may be any that keep to these rules, and one draw needn't show every extreme that they name: `pair_epochs`: each row names an earlier and a strictly later epoch; epoch 0 and epoch 150 - 1 both occur. inverse[e, k] = G[k, e] / (1 + the number of interferograms that name epoch e), rounded to bfloat16, where G[k, e] is 1 at later[k], -1 at earlier[k] and 0 elsewhere. `footprint`: offsets place a pixel in its own tile's 2 cells or in the next tile's; the pixels of the last tile of the strip lie in its own cells.
All inputs are finite; a program needn't handle non-finite values.
Results may differ from the reference program's by a relative error of at most 0.0033.
Values may be sent and summed in bfloat16 or wider, within the bound.
No kernel may reach another device: no remote copies, remote signals or barrier semaphores. Data moves between devices by JAX's collectives and lax.ppermute only.
A program may use at most 64 MiB of HBM per device.

```python
import jax
import jax.numpy as jnp
from jax import lax

TILE = 512
EPOCHS = 150
ITERS = 4
PAIRS = 640
SLABS = 128
SLAB_PIX = 1024
CT = 2
CELLS = 512
N_COL = 2


def network(key):
    first_key, second_key = jax.random.split(key)
    earlier = jax.random.randint(first_key, (PAIRS,), 0, EPOCHS - 1)
    spacing = jax.random.randint(second_key, (PAIRS,), 1, 7)
    order = jnp.arange(PAIRS, dtype=jnp.int32)
    earlier = jnp.where(order == 0, 0, earlier)
    later = jnp.minimum(earlier + spacing, EPOCHS - 1)
    later = jnp.where(order == PAIRS - 1, EPOCHS - 1, later)
    return jnp.stack([earlier, later], axis=1).astype(jnp.int32)


def draw_pair_epochs(key, part):
    return network(key)


def draw_inverse(key, part):
    pairs = network(key)
    epoch_index = jnp.arange(EPOCHS, dtype=jnp.int32)
    later_hit = (epoch_index[:, None] == pairs[None, :, 1]).astype(jnp.float32)
    earlier_hit = (epoch_index[:, None] == pairs[None, :, 0]).astype(jnp.float32)
    design_t = later_hit - earlier_hit
    degree = jnp.sum(later_hit + earlier_hit, axis=1, keepdims=True)
    return (design_t / (degree + 1.0)).astype(jnp.bfloat16)


def draw_footprint(key, part):
    key = jax.random.fold_in(key, 7)
    offsets = jax.random.randint(key, (SLABS, SLAB_PIX), 0, 2 * CT)
    slab_index = jnp.arange(SLABS, dtype=jnp.int32)[:, None]
    pixel_index = jnp.arange(SLAB_PIX, dtype=jnp.int32)[None, :]
    last_tile = (slab_index == SLABS - 1) & (pixel_index >= SLAB_PIX - TILE)
    return jnp.where(last_tile, offsets % CT, offsets).astype(jnp.int32)


def block_scale(key, dims, shards, smallest, largest):
    level, own = 1.0, jax.random.fold_in(key, 6)
    for axis_at, shards_of in shards:
        heights = jnp.exp(jax.random.uniform(jax.random.fold_in(own, axis_at), (shards_of,), jnp.float32, smallest / len(shards), largest / len(shards)))
        level = level * jnp.repeat(heights, dims[axis_at] // shards_of).reshape([-1 if axis == axis_at else 1 for axis in range(len(dims))])
    return level


def noise(key, shape, spread, limit, cuts=(), kind=jnp.bfloat16):
    factor_of = block_scale(key, shape, cuts, -0.22, 0.18) if cuts else 1.0
    array = jax.random.normal(key, shape, jnp.float32) * spread * factor_of
    return jnp.minimum(jnp.maximum(array, -limit), limit).astype(kind)


def setup_inputs(seed: int = 0) -> dict:
    arg_keys = jax.random.split(jax.random.key(seed), 6)
    interferograms = noise(arg_keys[0], (PAIRS, SLABS, SLAB_PIX), 2.0, 10.0, ((0, 128), (2, 2)))
    coherence = jnp.clip(0.099609375 + 0.9003906 * jax.random.uniform(arg_keys[1], (PAIRS, SLABS, SLAB_PIX), jnp.float32) ** block_scale(arg_keys[1], (PAIRS, SLABS, SLAB_PIX), ((0, 128), (2, 2)), -0.2, 0.2), 0.099609375, 1.0).astype(jnp.bfloat16)
    pair_epochs = draw_pair_epochs(jax.random.fold_in(arg_keys[5], 71), 0)
    inverse = draw_inverse(jax.random.fold_in(arg_keys[5], 71), 0)
    footprint = draw_footprint(jax.random.fold_in(arg_keys[5], 71), 0)
    return {"interferograms": interferograms, "coherence": coherence, "pair_epochs": pair_epochs, "inverse": inverse, "footprint": footprint}


phase_scale = 1.5


def residual_weights(motion, phases, quality, earlier, later):
    modeled = jnp.take(motion, later, axis=0) - jnp.take(motion, earlier, axis=0)
    residual = phases - modeled
    weight = quality / (1.0 + (residual / phase_scale) ** 2)
    return residual, weight


def reweighted_solve(phase_block, quality_block, pair_epochs, inverse):
    earlier = pair_epochs[:, 0]
    later = pair_epochs[:, 1]
    phases = phase_block.astype(jnp.float32)
    quality = quality_block.astype(jnp.float32)
    motion = jnp.zeros((inverse.shape[0], phase_block.shape[1]), jnp.float32)
    for repeat in range(ITERS):
        residual, weight = residual_weights(motion, phases, quality, earlier, later)
        weighted = (weight * residual).astype(jnp.bfloat16)
        motion = motion + jnp.dot(inverse, weighted, preferred_element_type=jnp.float32)
    residual, weight = residual_weights(motion, phases, quality, earlier, later)
    misfit = jnp.sum(weight * residual * residual, axis=0) / jnp.sum(weight, axis=0)
    return motion.astype(jnp.bfloat16), misfit


def bin_cells(rounded, offsets, window):
    targets = jnp.arange(window, dtype=jnp.int32)
    onehot = (targets[:, None] == offsets[None, :]).astype(jnp.bfloat16)
    return lax.dot_general(rounded, onehot, (((1,), (1,)), ((), ())), preferred_element_type=jnp.float32)


def reference(interferograms, coherence, pair_epochs, inverse, footprint):
    def one_slab(slab_index):
        phase_block = lax.dynamic_index_in_dim(interferograms, slab_index, 1, keepdims=False)
        quality_block = lax.dynamic_index_in_dim(coherence, slab_index, 1, keepdims=False)
        slab_offsets = lax.dynamic_index_in_dim(footprint, slab_index, 0, keepdims=False)
        rounded, misfit = reweighted_solve(phase_block, quality_block, pair_epochs, inverse)
        blocks = []
        for half_index in range(N_COL):
            columns = rounded[:, half_index * TILE:(half_index + 1) * TILE]
            offsets = slab_offsets[half_index * TILE:(half_index + 1) * TILE]
            blocks.append(bin_cells(columns, offsets, 2 * CT))
        return misfit, jnp.stack(blocks)

    misfit, partial_value = lax.map(one_slab, jnp.arange(SLABS, dtype=jnp.int32))
    partial_value = partial_value.reshape(SLABS * N_COL, EPOCHS, 2 * CT)
    own_cells = partial_value[:, :, :CT]
    spilled = partial_value[:, :, CT:]
    spilled_in = jnp.concatenate([jnp.zeros_like(spilled[:1]), spilled[:-1]], axis=0)
    volumes = (own_cells + spilled_in).transpose(1, 0, 2).reshape(EPOCHS, CELLS)
    return misfit, volumes
```

```python
import functools

import jax
import jax.numpy as jnp
from jax import lax
from jax.experimental import pallas as pl
from jax.experimental.pallas import tpu as pltpu
from jax.sharding import PartitionSpec as P

PPC = 256
ITERS = 4
LANES = 128
SUBLANES = 8
EPOCH_ROWS = 160
EPOCH_DEPTH = 256

phase_scale = 1.5
scale_squared = phase_scale**2


def from_behind(block, axis, distance):
    devices = range(lax.axis_size(axis))
    route = [(i - distance, i) for i in devices if i - distance in devices]
    return lax.ppermute(block, axis, route)


def pack_kernel(phase_ref, quality_ref, packed_ref, rows_ref):
    pairs, slabs, pixels = phase_ref.shape
    chunks = pixels // LANES
    block = pairs * 2 * chunks
    for group in range(slabs // 16):
        for k in range(pairs):
            for which, ref in enumerate((phase_ref, quality_ref)):
                for c in range(chunks):
                    tile = ref[k, pl.ds(group * 16, 16), pl.ds(c * LANES, LANES)].astype(jnp.float32)
                    row = k * 2 * chunks + which * chunks + c
                    for half in range(2):
                        first = (group * 16 + half * 8) * block + row
                        rows_ref[pl.ds(first, 8, stride=block), :] = tile[half * 8 : half * 8 + 8]
    for at in range(0, slabs * block, 16):
        packed_ref[pl.ds(at, 16), :] = rows_ref[pl.ds(at, 16), :].astype(jnp.bfloat16)


def pack(interferograms, coherence):
    pairs, slabs, pixels = interferograms.shape
    rows = slabs * pairs * 2 * pixels // LANES
    return pl.pallas_call(
        pack_kernel,
        out_shape=jax.ShapeDtypeStruct((rows, LANES), jnp.bfloat16),
        in_specs=[pl.BlockSpec(memory_space=pltpu.VMEM)] * 2,
        out_specs=pl.BlockSpec(memory_space=pltpu.VMEM),
        scratch_shapes=[pltpu.VMEM((rows, LANES), jnp.float32)],
        compiler_params=pltpu.CompilerParams(vmem_limit_bytes=16 << 20),
        name="pack",
    )(interferograms, coherence)


def prepare_kernel(named_ref, inverse_ref, design_ref, spread_ref):
    pairs = named_ref.shape[1]
    epochs = lax.broadcasted_iota(jnp.int32, (EPOCH_DEPTH, pairs), 0)
    later = (epochs == named_ref[1:2, :]).astype(jnp.float32)
    earlier = (epochs == named_ref[0:1, :]).astype(jnp.float32)
    design_ref[...] = (later - earlier).T.astype(jnp.bfloat16)
    spread_ref[...] = jnp.zeros_like(spread_ref)
    spread_ref[0 : inverse_ref.shape[0], :] = inverse_ref[...]


def prepare(pair_epochs, inverse):
    pairs = pair_epochs.shape[0]
    return pl.pallas_call(
        prepare_kernel,
        out_shape=(
            jax.ShapeDtypeStruct((pairs, EPOCH_DEPTH), jnp.bfloat16),
            jax.ShapeDtypeStruct((EPOCH_ROWS, pairs), jnp.bfloat16),
        ),
        in_specs=[pl.BlockSpec(memory_space=pltpu.VMEM)] * 2,
        out_specs=[pl.BlockSpec(memory_space=pltpu.VMEM)] * 2,
        compiler_params=pltpu.CompilerParams(vmem_limit_bytes=16 << 20),
        name="prepare",
    )(pair_epochs.T, inverse)


def solve_kernel(
    received_ref, design_ref, spread_ref, footprint_ref, misfit_ref, cells_ref,
    rows_ref, phase_ref, quality_ref, motion_ref, high_ref, low_ref,
):
    pairs, pixels = phase_ref.shape
    chunks = pixels // LANES
    deep = 128
    for at in range(0, rows_ref.shape[0], 16):
        rows_ref[pl.ds(at, 16), :] = received_ref[pl.ds(at, 16), :].astype(jnp.float32)

    def first_block(k0):
        parts = []
        for c in range(chunks):
            column = []
            for k in range(k0, k0 + deep, 8):
                phase = rows_ref[pl.ds(k * 8 + c, 8, stride=8), :]
                quality = rows_ref[pl.ds(k * 8 + chunks + c, 8, stride=8), :] * scale_squared
                phase_ref[pl.ds(k, 8), pl.ds(c * LANES, LANES)] = phase
                quality_ref[pl.ds(k, 8), pl.ds(c * LANES, LANES)] = quality
                column.append(quality * phase / (scale_squared + phase * phase))
            parts.append(jnp.concatenate(column, axis=0))
        return jnp.concatenate(parts, axis=1).astype(jnp.bfloat16)

    def modeled(k0):
        design = design_ref[pl.ds(k0, deep), :]
        return jnp.dot(design, high_ref[...], preferred_element_type=jnp.float32) + jnp.dot(
            design, low_ref[...], preferred_element_type=jnp.float32
        )

    def block_weights(k0):
        residual = phase_ref[pl.ds(k0, deep), :] - modeled(k0)
        square = residual * residual
        weight = quality_ref[pl.ds(k0, deep), :] / (scale_squared + square)
        return residual, square, weight

    def keep(motion):
        motion_ref[...] = motion
        high = motion.astype(jnp.bfloat16)
        high_ref[0:EPOCH_ROWS, :] = high
        low_ref[0:EPOCH_ROWS, :] = (motion - high.astype(jnp.float32)).astype(jnp.bfloat16)

    high_ref[...] = jnp.zeros_like(high_ref)
    low_ref[...] = jnp.zeros_like(low_ref)
    for repeat in range(ITERS):
        change = jnp.zeros((EPOCH_ROWS, pixels), jnp.float32)
        for k0 in range(0, pairs, deep):
            if repeat == 0:
                weighted = first_block(k0)
            else:
                residual, _, weight = block_weights(k0)
                weighted = (weight * residual).astype(jnp.bfloat16)
            change += jnp.dot(
                spread_ref[:, pl.ds(k0, deep)], weighted, preferred_element_type=jnp.float32
            )
        keep(change if repeat == 0 else motion_ref[...] + change)

    targets = lax.broadcasted_iota(jnp.int32, (SUBLANES, pixels), 0)
    onehot = (targets == footprint_ref[...]).astype(jnp.bfloat16)
    cells_ref[...] = lax.dot_general(
        onehot, high_ref[...], (((1,), (1,)), ((), ())), preferred_element_type=jnp.float32
    )

    above = jnp.zeros((SUBLANES, pixels), jnp.float32)
    below = jnp.zeros((SUBLANES, pixels), jnp.float32)
    for k0 in range(0, pairs, deep):
        _, square, weight = block_weights(k0)
        above += jnp.sum((weight * square).reshape(deep // 8, 8, pixels), axis=0)
        below += jnp.sum(weight.reshape(deep // 8, 8, pixels), axis=0)
    misfit_ref[...] = jnp.sum(above, axis=0, keepdims=True) / jnp.sum(below, axis=0, keepdims=True)


def solve(received, design, spread, footprint):
    pairs = design.shape[0]
    pixels = footprint.shape[1]
    return pl.pallas_call(
        solve_kernel,
        out_shape=(
            jax.ShapeDtypeStruct((1, pixels), jnp.float32),
            jax.ShapeDtypeStruct((SUBLANES, EPOCH_DEPTH), jnp.float32),
        ),
        in_specs=[pl.BlockSpec(memory_space=pltpu.VMEM)] * 4,
        out_specs=[pl.BlockSpec(memory_space=pltpu.VMEM)] * 2,
        scratch_shapes=[
            pltpu.VMEM(received.shape, jnp.float32),
            pltpu.VMEM((pairs, pixels), jnp.float32),
            pltpu.VMEM((pairs, pixels), jnp.float32),
            pltpu.VMEM((EPOCH_ROWS, pixels), jnp.float32),
            pltpu.VMEM((EPOCH_DEPTH, pixels), jnp.bfloat16),
            pltpu.VMEM((EPOCH_DEPTH, pixels), jnp.bfloat16),
        ],
        compiler_params=pltpu.CompilerParams(vmem_limit_bytes=24 << 20),
        name="solve",
    )(received, design, spread, footprint)


def body(interferograms, coherence, pair_epochs, inverse, footprint):
    slabs = lax.axis_size("pair")
    packed = pack(interferograms, coherence)
    blocks = packed.reshape(slabs, packed.shape[0] // slabs, LANES)
    blocks = lax.all_to_all(blocks, "pair", split_axis=0, concat_axis=0, tiled=True)
    received = blocks.reshape(packed.shape)
    design, spread = prepare(pair_epochs, inverse)
    misfit, cells = solve(received, design, spread, footprint)
    cells_tile = footprint.shape[1] // PPC
    epochs = inverse.shape[0]
    own_cells = cells[:cells_tile, :epochs]
    spilled = cells[cells_tile : 2 * cells_tile, :epochs]
    arrived = from_behind(spilled, ("pair", "col"), 1)
    return (misfit, (own_cells + arrived).T)


def solution(mesh):
    in_specs = (P("pair", None, "col"), P("pair", None, "col"), P(), P(), P("pair", "col"))
    out_specs = (P("pair", "col"), P(None, ("pair", "col")))
    return jax.shard_map(body, mesh=mesh, in_specs=in_specs, out_specs=out_specs, check_vma=False)
```

```python
import jax
import jax.numpy as jnp
import numpy as np
from jax import lax
from jax.experimental import pallas as pl
from jax.experimental.pallas import tpu as pltpu
from jax.sharding import PartitionSpec as P

PPC = 256
ITERS = 4
LANES = 128
SUBLANES = 8
GROUP = 16
EPOCH_ROWS = 160
EPOCH_DEPTH = 256
HALF = 256
ORDER_SEED = 102

phase_scale = 1.5
scale_squared = phase_scale**2

VMEM = pl.BlockSpec(memory_space=pltpu.VMEM)
HBM = pl.BlockSpec(memory_space=pltpu.HBM)


def exchange_order(devices):
    halves = np.random.RandomState(ORDER_SEED).permutation(devices // 2)
    return [int(2 * half + side) for half in halves for side in range(2)]


def from_behind(block, axis, distance):
    devices = range(lax.axis_size(axis))
    route = [(i - distance, i) for i in devices if i - distance in devices]
    return lax.ppermute(block, axis, route)


def swap_rows(outer, scale_late):
    inner = LANES // outer
    row = lax.broadcasted_iota(jnp.int32, (LANES, LANES), 0)
    column = lax.broadcasted_iota(jnp.int32, (LANES, LANES), 1)
    hit = (row // inner == column % outer) & (row % inner == column // outer)
    value = jnp.where(row >= LANES // 2, scale_late, 1.0)
    return jnp.where(hit, value, 0.0).astype(jnp.bfloat16)


def pack_kernel(order, phase_hbm, quality_hbm, packed_ref, phase_ref, quality_ref, sems):
    pairs, slabs, pixels = phase_ref.shape
    step = slabs // sems.shape[0]
    copies = []
    for part in range(sems.shape[0]):
        for which, (source, target) in enumerate(((phase_hbm, phase_ref), (quality_hbm, quality_ref))):
            span = pl.ds(part * step, step)
            copies.append(
                pltpu.make_async_copy(source.at[:, span, :], target.at[:, span, :], sems.at[part, which])
            )
            copies[-1].start()
    place = {slab: at for at, slab in enumerate(order)}
    swap = swap_rows(GROUP, 1.0)
    for group in range(slabs // GROUP):
        if group * GROUP % step == 0:
            for copy in copies[2 * (group * GROUP // step) :][:2]:
                copy.wait()
        rows = [
            jnp.concatenate(
                [ref[k, pl.ds(group * GROUP, GROUP), pl.ds(c * LANES, LANES)] for k in range(pairs)], axis=1
            )
            for ref in (phase_ref, quality_ref)
            for c in range(pixels // LANES)
        ]
        swapped = jnp.dot(swap, jnp.concatenate(rows, axis=0), preferred_element_type=jnp.float32)
        for slab in range(0, GROUP, 2):
            tiles = [
                swapped[s * SUBLANES : (s + 1) * SUBLANES, k * LANES : (k + 1) * LANES]
                for s in (slab, slab + 1)
                for k in range(pairs)
            ]
            first = place[group * GROUP + slab] * pairs * SUBLANES
            for at in range(0, len(tiles), 2):
                packed_ref[pl.ds(first + at * SUBLANES, 2 * SUBLANES), :] = jnp.concatenate(
                    tiles[at : at + 2], axis=0
                ).astype(jnp.bfloat16)


def pack(interferograms, coherence, order):
    pairs, slabs, pixels = interferograms.shape
    rows = slabs * pairs * 2 * pixels // LANES
    return pl.pallas_call(
        lambda *refs: pack_kernel(order, *refs),
        out_shape=jax.ShapeDtypeStruct((rows, LANES), jnp.bfloat16),
        in_specs=[HBM] * 2,
        out_specs=VMEM,
        scratch_shapes=[
            pltpu.VMEM(interferograms.shape, jnp.bfloat16),
            pltpu.VMEM(coherence.shape, jnp.bfloat16),
            pltpu.SemaphoreType.DMA((2, 2)),
        ],
        compiler_params=pltpu.CompilerParams(vmem_limit_bytes=60 << 20),
        name="pack",
    )(interferograms, coherence)


def prepare_kernel(arrival_ref, named_ref, inverse_ref, design_ref, spread_ref):
    pairs = named_ref.shape[1]
    reorder = (lax.broadcasted_iota(jnp.int32, (pairs, pairs), 0) == arrival_ref[...]).astype(jnp.bfloat16)
    named = jnp.dot(
        named_ref[...].astype(jnp.float32).astype(jnp.bfloat16), reorder, preferred_element_type=jnp.float32
    )
    epochs = lax.broadcasted_iota(jnp.int32, (EPOCH_DEPTH, pairs), 0).astype(jnp.float32)
    later = (epochs == named[1:2, :]).astype(jnp.float32)
    earlier = (epochs == named[0:1, :]).astype(jnp.float32)
    design = (later - earlier).T.astype(jnp.bfloat16)
    design_ref[:, 0:EPOCH_DEPTH] = design
    design_ref[:, EPOCH_DEPTH:] = design
    spread = jnp.dot(inverse_ref[...], reorder, preferred_element_type=jnp.float32).astype(jnp.bfloat16)
    spread_ref[...] = jnp.zeros_like(spread_ref)
    spread_ref[0 : inverse_ref.shape[0], :] = spread


def prepare(pair_epochs, inverse, arrival):
    pairs = pair_epochs.shape[0]
    return pl.pallas_call(
        prepare_kernel,
        out_shape=(
            jax.ShapeDtypeStruct((pairs, 2 * EPOCH_DEPTH), jnp.bfloat16),
            jax.ShapeDtypeStruct((EPOCH_ROWS, pairs), jnp.bfloat16),
        ),
        in_specs=[VMEM] * 3,
        out_specs=[VMEM] * 2,
        compiler_params=pltpu.CompilerParams(vmem_limit_bytes=16 << 20),
        name="prepare",
    )(arrival, pair_epochs.T, inverse)


def sweeps_kernel(
    received_ref, design_ref, spread_ref, footprint_ref, cells_ref, phase_ref, quality_ref, parts_ref,
    motion_ref, weighted_ref, modeled_ref,
):
    pairs, pixels = phase_ref.shape
    chunks = pixels // LANES
    swap = swap_rows(SUBLANES, scale_squared)
    for group in range(0, pairs // GROUP, 2):
        taken = [received_ref[pl.ds((group + side) * LANES, LANES), :] for side in range(2)]
        swapped = jnp.dot(swap, jnp.concatenate(taken, axis=1), preferred_element_type=jnp.float32)
        for side in range(2):
            lanes = swapped[:, side * LANES : (side + 1) * LANES]
            for c in range(chunks):
                rows, columns = pl.ds((group + side) * GROUP, GROUP), pl.ds(c * LANES, LANES)
                phase = lanes[c * GROUP : (c + 1) * GROUP]
                quality = lanes[(chunks + c) * GROUP : (chunks + c + 1) * GROUP]
                phase_ref[rows, columns] = phase
                quality_ref[rows, columns] = quality
                weighted_ref[rows, columns] = (quality * phase / (scale_squared + phase * phase)).astype(
                    jnp.bfloat16
                )
    parts_ref[...] = jnp.zeros_like(parts_ref)
    for repeat in range(ITERS):
        for half in range(0, pixels, HALF):
            columns = pl.ds(half, HALF)
            if repeat > 0:
                for k in range(0, pairs, LANES):
                    rows = pl.ds(k, LANES)
                    residual = phase_ref[rows, columns] - modeled_ref[rows, columns]
                    weighted_ref[rows, columns] = (
                        quality_ref[rows, columns] * residual / (scale_squared + residual * residual)
                    ).astype(jnp.bfloat16)
            motion = jnp.dot(spread_ref[...], weighted_ref[:, columns], preferred_element_type=jnp.float32)
            if repeat > 0:
                motion = motion_ref[:, columns] + motion
            motion_ref[:, columns] = motion
            high = motion.astype(jnp.bfloat16)
            parts_ref[0:EPOCH_ROWS, columns] = high
            parts_ref[EPOCH_DEPTH : EPOCH_DEPTH + EPOCH_ROWS, columns] = (
                motion - high.astype(jnp.float32)
            ).astype(jnp.bfloat16)
            if repeat < ITERS - 1:
                modeled_ref[:, columns] = jnp.dot(
                    design_ref[...], parts_ref[:, columns], preferred_element_type=jnp.float32
                )
    targets = lax.broadcasted_iota(jnp.int32, (SUBLANES, pixels), 0)
    onehot = (targets == footprint_ref[...]).astype(jnp.bfloat16)
    cells_ref[...] = lax.dot_general(
        onehot, parts_ref[0:EPOCH_DEPTH, :], (((1,), (1,)), ((), ())), preferred_element_type=jnp.float32
    )


def sweeps(received, design, spread, footprint):
    pairs = design.shape[0]
    pixels = footprint.shape[1]
    return pl.pallas_call(
        sweeps_kernel,
        out_shape=(
            jax.ShapeDtypeStruct((SUBLANES, EPOCH_DEPTH), jnp.float32),
            jax.ShapeDtypeStruct((pairs, pixels), jnp.float32),
            jax.ShapeDtypeStruct((pairs, pixels), jnp.float32),
            jax.ShapeDtypeStruct((2 * EPOCH_DEPTH, pixels), jnp.bfloat16),
        ),
        in_specs=[VMEM] * 4,
        out_specs=[VMEM] * 4,
        scratch_shapes=[
            pltpu.VMEM((EPOCH_ROWS, pixels), jnp.float32),
            pltpu.VMEM((pairs, pixels), jnp.bfloat16),
            pltpu.VMEM((pairs, pixels), jnp.float32),
        ],
        compiler_params=pltpu.CompilerParams(vmem_limit_bytes=24 << 20),
        name="sweeps",
    )(received, design, spread, footprint)


def misfit_kernel(design_ref, phase_ref, quality_ref, parts_ref, misfit_ref, modeled_ref):
    pairs, pixels = phase_ref.shape
    for half in range(0, pixels, HALF):
        columns = pl.ds(half, HALF)
        modeled_ref[:, columns] = jnp.dot(
            design_ref[...], parts_ref[:, columns], preferred_element_type=jnp.float32
        )
    for half in range(0, pixels, HALF):
        columns = pl.ds(half, HALF)
        above = jnp.zeros((SUBLANES, HALF), jnp.float32)
        below = jnp.zeros((SUBLANES, HALF), jnp.float32)
        for k in range(0, pairs, SUBLANES):
            rows = pl.ds(k, SUBLANES)
            residual = phase_ref[rows, columns] - modeled_ref[rows, columns]
            square = residual * residual
            weight = quality_ref[rows, columns] / (scale_squared + square)
            above += weight * square
            below += weight
        misfit_ref[:, columns] = jnp.sum(above, axis=0, keepdims=True) / jnp.sum(below, axis=0, keepdims=True)


def misfits(design, phase, quality, parts):
    pairs, pixels = phase.shape
    return pl.pallas_call(
        misfit_kernel,
        out_shape=jax.ShapeDtypeStruct((1, pixels), jnp.float32),
        in_specs=[VMEM] * 4,
        out_specs=VMEM,
        scratch_shapes=[pltpu.VMEM((pairs, pixels), jnp.float32)],
        compiler_params=pltpu.CompilerParams(vmem_limit_bytes=24 << 20),
        name="misfit",
    )(design, phase, quality, parts)


def body(interferograms, coherence, pair_epochs, inverse, footprint):
    devices = lax.axis_size("pair")
    order = exchange_order(devices)
    packed = pack(interferograms, coherence, order)
    blocks = lax.all_to_all(
        packed.reshape(devices, packed.shape[0] // devices, LANES),
        "pair",
        split_axis=0,
        concat_axis=0,
        tiled=True,
        axis_index_groups=[order],
    )
    local = interferograms.shape[0]
    arrival = np.array([[device * local + k for device in order for k in range(local)]], np.int32)
    design, spread = prepare(pair_epochs, inverse, jnp.asarray(arrival))
    cells, phase, quality, parts = sweeps(blocks.reshape(packed.shape), design, spread, footprint)
    cells_tile = footprint.shape[1] // PPC
    epochs = inverse.shape[0]
    own_cells = cells[:cells_tile, :epochs]
    spilled = cells[cells_tile : 2 * cells_tile, :epochs]
    arrived = from_behind(spilled, ("pair", "col"), 1)
    misfit = misfits(design, phase, quality, parts)
    return (misfit, (own_cells + arrived).T)


def solution(mesh):
    in_specs = (P("pair", None, "col"), P("pair", None, "col"), P(), P(), P("pair", "col"))
    out_specs = (P("pair", "col"), P(None, ("pair", "col")))
    return jax.shard_map(body, mesh=mesh, in_specs=in_specs, out_specs=out_specs, check_vma=False)
```

```python
import jax
import jax.numpy as jnp
import numpy as np
from jax import lax
from jax.experimental import pallas as pl
from jax.experimental.pallas import tpu as pltpu
from jax.sharding import PartitionSpec as P

PPC = 256
ITERS = 4
LANES = 128
SUBLANES = 8
GROUP = 16
EPOCH_ROWS = 160
EPOCH_DEPTH = 256
HALF = 256
ORDER_SEED = 121

phase_scale = 1.5
scale_squared = phase_scale**2

VMEM = pl.BlockSpec(memory_space=pltpu.VMEM)
HBM = pl.BlockSpec(memory_space=pltpu.HBM)


def exchange_order(devices):
    halves = np.random.RandomState(ORDER_SEED).permutation(devices // 2)
    return [int(2 * half + side) for half in halves for side in range(2)]


def from_behind(block, axis, distance):
    devices = range(lax.axis_size(axis))
    route = [(i - distance, i) for i in devices if i - distance in devices]
    return lax.ppermute(block, axis, route)


def swap_rows(outer, scale_late):
    inner = LANES // outer
    row = lax.broadcasted_iota(jnp.int32, (LANES, LANES), 0)
    column = lax.broadcasted_iota(jnp.int32, (LANES, LANES), 1)
    hit = (row // inner == column % outer) & (row % inner == column // outer)
    value = jnp.where(row >= LANES // 2, scale_late, 1.0)
    return jnp.where(hit, value, 0.0).astype(jnp.bfloat16)


def reorder_pairs(arrival_ref, named_ref, inverse_ref, design_ref, spread_ref):
    pairs = named_ref.shape[1]
    reorder = (lax.broadcasted_iota(jnp.int32, (pairs, pairs), 0) == arrival_ref[...]).astype(jnp.bfloat16)
    named = jnp.dot(
        named_ref[...].astype(jnp.float32).astype(jnp.bfloat16), reorder, preferred_element_type=jnp.float32
    )
    epochs = lax.broadcasted_iota(jnp.int32, (EPOCH_DEPTH, pairs), 0).astype(jnp.float32)
    later = (epochs == named[1:2, :]).astype(jnp.float32)
    earlier = (epochs == named[0:1, :]).astype(jnp.float32)
    design = (later - earlier).T.astype(jnp.bfloat16)
    design_ref[:, 0:EPOCH_DEPTH] = design
    design_ref[:, EPOCH_DEPTH:] = design
    spread = jnp.dot(inverse_ref[...], reorder, preferred_element_type=jnp.float32).astype(jnp.bfloat16)
    spread_ref[...] = jnp.zeros_like(spread_ref)
    spread_ref[0 : inverse_ref.shape[0], :] = spread


def pack_kernel(
    order, phase_hbm, quality_hbm, arrival_hbm, named_hbm, inverse_hbm, packed_ref, design_ref, spread_ref,
    phase_ref, quality_ref, arrival_ref, named_ref, inverse_ref, small_sems, sems,
):
    pairs, slabs, pixels = phase_ref.shape
    step = slabs // sems.shape[0]
    small = [
        pltpu.make_async_copy(source, target, small_sems.at[at])
        for at, (source, target) in enumerate(
            ((arrival_hbm, arrival_ref), (named_hbm, named_ref), (inverse_hbm, inverse_ref))
        )
    ]
    large = []
    for part in range(sems.shape[0]):
        for which, (source, target) in enumerate(((phase_hbm, phase_ref), (quality_hbm, quality_ref))):
            span = pl.ds(part * step, step)
            large.append(
                pltpu.make_async_copy(source.at[:, span, :], target.at[:, span, :], sems.at[part, which])
            )
    for copy in small + large:
        copy.start()
    for copy in small:
        copy.wait()
    reorder_pairs(arrival_ref, named_ref, inverse_ref, design_ref, spread_ref)
    place = {slab: at for at, slab in enumerate(order)}
    swap = swap_rows(GROUP, 1.0)
    for group in range(slabs // GROUP):
        if group * GROUP % step == 0:
            for copy in large[2 * (group * GROUP // step) :][:2]:
                copy.wait()
        rows = [
            jnp.concatenate(
                [ref[k, pl.ds(group * GROUP, GROUP), pl.ds(c * LANES, LANES)] for k in range(pairs)], axis=1
            )
            for ref in (phase_ref, quality_ref)
            for c in range(pixels // LANES)
        ]
        swapped = jnp.dot(swap, jnp.concatenate(rows, axis=0), preferred_element_type=jnp.float32)
        for slab in range(0, GROUP, 2):
            tiles = [
                swapped[s * SUBLANES : (s + 1) * SUBLANES, k * LANES : (k + 1) * LANES]
                for s in (slab, slab + 1)
                for k in range(pairs)
            ]
            first = place[group * GROUP + slab] * pairs * SUBLANES
            for at in range(0, len(tiles), 2):
                packed_ref[pl.ds(first + at * SUBLANES, 2 * SUBLANES), :] = jnp.concatenate(
                    tiles[at : at + 2], axis=0
                ).astype(jnp.bfloat16)


def pack(interferograms, coherence, pair_epochs, inverse, order):
    pairs, slabs, pixels = interferograms.shape
    rows = slabs * pairs * 2 * pixels // LANES
    arrival = np.array([[device * pairs + k for device in order for k in range(pairs)]], np.int32)
    taken = (interferograms, coherence, jnp.asarray(arrival), pair_epochs.T, inverse)
    return pl.pallas_call(
        lambda *refs: pack_kernel(order, *refs),
        out_shape=(
            jax.ShapeDtypeStruct((rows, LANES), jnp.bfloat16),
            jax.ShapeDtypeStruct((arrival.shape[1], 2 * EPOCH_DEPTH), jnp.bfloat16),
            jax.ShapeDtypeStruct((EPOCH_ROWS, arrival.shape[1]), jnp.bfloat16),
        ),
        in_specs=[HBM] * len(taken),
        out_specs=[VMEM] * 3,
        scratch_shapes=[pltpu.VMEM(array.shape, array.dtype) for array in taken]
        + [pltpu.SemaphoreType.DMA((3,)), pltpu.SemaphoreType.DMA((2, 2))],
        compiler_params=pltpu.CompilerParams(vmem_limit_bytes=24 << 20),
        name="pack",
    )(*(pltpu.with_memory_space_constraint(array, pltpu.HBM) for array in taken))


def sweeps_kernel(
    received_ref, design_ref, spread_ref, footprint_ref, cells_ref, phase_ref, quality_ref, parts_ref,
    motion_ref, weighted_ref, modeled_ref,
):
    pairs, pixels = phase_ref.shape
    chunks = pixels // LANES
    swap = swap_rows(SUBLANES, scale_squared)
    for group in range(0, pairs // GROUP, 2):
        taken = [received_ref[pl.ds((group + side) * LANES, LANES), :] for side in range(2)]
        swapped = jnp.dot(swap, jnp.concatenate(taken, axis=1), preferred_element_type=jnp.float32)
        for side in range(2):
            lanes = swapped[:, side * LANES : (side + 1) * LANES]
            for c in range(chunks):
                rows, columns = pl.ds((group + side) * GROUP, GROUP), pl.ds(c * LANES, LANES)
                phase = lanes[c * GROUP : (c + 1) * GROUP]
                quality = lanes[(chunks + c) * GROUP : (chunks + c + 1) * GROUP]
                phase_ref[rows, columns] = phase
                quality_ref[rows, columns] = quality
                weighted_ref[rows, columns] = (quality * phase / (scale_squared + phase * phase)).astype(
                    jnp.bfloat16
                )
    parts_ref[...] = jnp.zeros_like(parts_ref)
    for repeat in range(ITERS):
        for half in range(0, pixels, HALF):
            columns = pl.ds(half, HALF)
            if repeat > 0:
                for k in range(0, pairs, LANES):
                    rows = pl.ds(k, LANES)
                    residual = phase_ref[rows, columns] - modeled_ref[rows, columns]
                    weighted_ref[rows, columns] = (
                        quality_ref[rows, columns] * residual / (scale_squared + residual * residual)
                    ).astype(jnp.bfloat16)
            motion = jnp.dot(spread_ref[...], weighted_ref[:, columns], preferred_element_type=jnp.float32)
            if repeat > 0:
                motion = motion_ref[:, columns] + motion
            motion_ref[:, columns] = motion
            high = motion.astype(jnp.bfloat16)
            parts_ref[0:EPOCH_ROWS, columns] = high
            parts_ref[EPOCH_DEPTH : EPOCH_DEPTH + EPOCH_ROWS, columns] = (
                motion - high.astype(jnp.float32)
            ).astype(jnp.bfloat16)
            if repeat < ITERS - 1:
                modeled_ref[:, columns] = jnp.dot(
                    design_ref[...], parts_ref[:, columns], preferred_element_type=jnp.float32
                )
    targets = lax.broadcasted_iota(jnp.int32, (SUBLANES, pixels), 0)
    onehot = (targets == footprint_ref[...]).astype(jnp.bfloat16)
    cells_ref[...] = lax.dot_general(
        onehot, parts_ref[0:EPOCH_DEPTH, :], (((1,), (1,)), ((), ())), preferred_element_type=jnp.float32
    )


def sweeps(received, design, spread, footprint):
    pairs = design.shape[0]
    pixels = footprint.shape[1]
    return pl.pallas_call(
        sweeps_kernel,
        out_shape=(
            jax.ShapeDtypeStruct((SUBLANES, EPOCH_DEPTH), jnp.float32),
            jax.ShapeDtypeStruct((pairs, pixels), jnp.float32),
            jax.ShapeDtypeStruct((pairs, pixels), jnp.float32),
            jax.ShapeDtypeStruct((2 * EPOCH_DEPTH, pixels), jnp.bfloat16),
        ),
        in_specs=[VMEM] * 4,
        out_specs=[VMEM] * 4,
        scratch_shapes=[
            pltpu.VMEM((EPOCH_ROWS, pixels), jnp.float32),
            pltpu.VMEM((pairs, pixels), jnp.bfloat16),
            pltpu.VMEM((pairs, pixels), jnp.float32),
        ],
        compiler_params=pltpu.CompilerParams(vmem_limit_bytes=24 << 20),
        name="sweeps",
    )(received, design, spread, footprint)


def misfit_kernel(design_ref, phase_ref, quality_ref, parts_ref, misfit_ref, modeled_ref):
    pairs, pixels = phase_ref.shape
    for half in range(0, pixels, HALF):
        columns = pl.ds(half, HALF)
        modeled_ref[:, columns] = jnp.dot(
            design_ref[...], parts_ref[:, columns], preferred_element_type=jnp.float32
        )
    for half in range(0, pixels, HALF):
        columns = pl.ds(half, HALF)
        above = jnp.zeros((SUBLANES, HALF), jnp.float32)
        below = jnp.zeros((SUBLANES, HALF), jnp.float32)
        for k in range(0, pairs, SUBLANES):
            rows = pl.ds(k, SUBLANES)
            residual = phase_ref[rows, columns] - modeled_ref[rows, columns]
            square = residual * residual
            weight = quality_ref[rows, columns] / (scale_squared + square)
            above += weight * square
            below += weight
        misfit_ref[:, columns] = jnp.sum(above, axis=0, keepdims=True) / jnp.sum(below, axis=0, keepdims=True)


def misfits(design, phase, quality, parts):
    pairs, pixels = phase.shape
    return pl.pallas_call(
        misfit_kernel,
        out_shape=jax.ShapeDtypeStruct((1, pixels), jnp.float32),
        in_specs=[VMEM] * 4,
        out_specs=VMEM,
        scratch_shapes=[pltpu.VMEM((pairs, pixels), jnp.float32)],
        compiler_params=pltpu.CompilerParams(vmem_limit_bytes=24 << 20),
        name="misfit",
    )(design, phase, quality, parts)


def body(interferograms, coherence, pair_epochs, inverse, footprint):
    devices = lax.axis_size("pair")
    order = exchange_order(devices)
    packed, design, spread = pack(interferograms, coherence, pair_epochs, inverse, order)
    blocks = lax.all_to_all(
        packed.reshape(devices, packed.shape[0] // devices, LANES),
        "pair",
        split_axis=0,
        concat_axis=0,
        tiled=True,
        axis_index_groups=[order],
    )
    cells, phase, quality, parts = sweeps(blocks.reshape(packed.shape), design, spread, footprint)
    cells_tile = footprint.shape[1] // PPC
    epochs = inverse.shape[0]
    own_cells = cells[:cells_tile, :epochs]
    spilled = cells[cells_tile : 2 * cells_tile, :epochs]
    arrived = from_behind(spilled, ("pair", "col"), 1)
    misfit = misfits(design, phase, quality, parts)
    return (misfit, (own_cells + arrived).T)


def solution(mesh):
    in_specs = (P("pair", None, "col"), P("pair", None, "col"), P(), P(), P("pair", "col"))
    out_specs = (P("pair", "col"), P(None, ("pair", "col")))
    return jax.shard_map(body, mesh=mesh, in_specs=in_specs, out_specs=out_specs, check_vma=False)
```

```python
import jax
import jax.numpy as jnp
import numpy as np
from jax import lax
from jax.experimental import pallas as pl
from jax.experimental.pallas import tpu as pltpu
from jax.sharding import PartitionSpec as P

PPC = 256
ITERS = 4
LANES = 128
SUBLANES = 8
GROUP = 16
EPOCH_ROWS = 160
EPOCH_DEPTH = 256
HALF = 256
ORDER_SEED = 121

phase_scale = 1.5
scale_squared = phase_scale**2

VMEM = pl.BlockSpec(memory_space=pltpu.VMEM)
HBM = pl.BlockSpec(memory_space=pltpu.HBM)


def exchange_order(devices):
    halves = np.random.RandomState(ORDER_SEED).permutation(devices // 2)
    return [int(2 * half + side) for half in halves for side in range(2)]


def from_behind(block, axis, distance):
    devices = range(lax.axis_size(axis))
    route = [(i - distance, i) for i in devices if i - distance in devices]
    return lax.ppermute(block, axis, route)


def swap_rows(outer, scale_late):
    inner = LANES // outer
    row = lax.broadcasted_iota(jnp.int32, (LANES, LANES), 0)
    column = lax.broadcasted_iota(jnp.int32, (LANES, LANES), 1)
    hit = (row // inner == column % outer) & (row % inner == column // outer)
    value = jnp.where(row >= LANES // 2, scale_late, 1.0)
    return jnp.where(hit, value, 0.0).astype(jnp.bfloat16)


def reorder_pairs(arrival_ref, named_ref, inverse_ref, design_ref, spread_ref):
    pairs = named_ref.shape[1]
    reorder = (lax.broadcasted_iota(jnp.int32, (pairs, pairs), 0) == arrival_ref[...]).astype(jnp.bfloat16)
    named = jnp.dot(
        named_ref[...].astype(jnp.float32).astype(jnp.bfloat16), reorder, preferred_element_type=jnp.float32
    )
    epochs = lax.broadcasted_iota(jnp.int32, (EPOCH_DEPTH, pairs), 0).astype(jnp.float32)
    later = (epochs == named[1:2, :]).astype(jnp.float32)
    earlier = (epochs == named[0:1, :]).astype(jnp.float32)
    design = (later - earlier).T.astype(jnp.bfloat16)
    design_ref[:, 0:EPOCH_DEPTH] = design
    design_ref[:, EPOCH_DEPTH:] = design
    spread = jnp.dot(inverse_ref[...], reorder, preferred_element_type=jnp.float32).astype(jnp.bfloat16)
    spread_ref[...] = jnp.zeros_like(spread_ref)
    spread_ref[0 : inverse_ref.shape[0], :] = spread


def pack_kernel(
    order, phase_hbm, quality_hbm, arrival_hbm, named_hbm, inverse_hbm, packed_ref, design_ref, spread_ref,
    phase_ref, quality_ref, arrival_ref, named_ref, inverse_ref, small_sems, sems,
):
    pairs, slabs, pixels = phase_ref.shape
    step = slabs // sems.shape[0]
    small = [
        pltpu.make_async_copy(source, target, small_sems.at[at])
        for at, (source, target) in enumerate(
            ((arrival_hbm, arrival_ref), (named_hbm, named_ref), (inverse_hbm, inverse_ref))
        )
    ]
    large = []
    for part in range(sems.shape[0]):
        for which, (source, target) in enumerate(((phase_hbm, phase_ref), (quality_hbm, quality_ref))):
            span = pl.ds(part * step, step)
            large.append(
                pltpu.make_async_copy(source.at[:, span, :], target.at[:, span, :], sems.at[part, which])
            )
    for copy in small + large:
        copy.start()
    for copy in small:
        copy.wait()
    reorder_pairs(arrival_ref, named_ref, inverse_ref, design_ref, spread_ref)
    place = {slab: at for at, slab in enumerate(order)}
    swap = swap_rows(GROUP, 1.0)
    for group in range(slabs // GROUP):
        if group * GROUP % step == 0:
            for copy in large[2 * (group * GROUP // step) :][:2]:
                copy.wait()
        rows = [
            jnp.concatenate(
                [ref[k, pl.ds(group * GROUP, GROUP), pl.ds(c * LANES, LANES)] for k in range(pairs)], axis=1
            )
            for ref in (phase_ref, quality_ref)
            for c in range(pixels // LANES)
        ]
        swapped = jnp.dot(swap, jnp.concatenate(rows, axis=0), preferred_element_type=jnp.float32)
        for slab in range(0, GROUP, 2):
            tiles = [
                swapped[s * SUBLANES : (s + 1) * SUBLANES, k * LANES : (k + 1) * LANES]
                for s in (slab, slab + 1)
                for k in range(pairs)
            ]
            first = place[group * GROUP + slab] * pairs * SUBLANES
            for at in range(0, len(tiles), 2):
                packed_ref[pl.ds(first + at * SUBLANES, 2 * SUBLANES), :] = jnp.concatenate(
                    tiles[at : at + 2], axis=0
                ).astype(jnp.bfloat16)


def pack(interferograms, coherence, pair_epochs, inverse, order):
    pairs, slabs, pixels = interferograms.shape
    rows = slabs * pairs * 2 * pixels // LANES
    arrival = np.array([[device * pairs + k for device in order for k in range(pairs)]], np.int32)
    taken = (interferograms, coherence, jnp.asarray(arrival), pair_epochs.T, inverse)
    return pl.pallas_call(
        lambda *refs: pack_kernel(order, *refs),
        out_shape=(
            jax.ShapeDtypeStruct((rows, LANES), jnp.bfloat16),
            jax.ShapeDtypeStruct((arrival.shape[1], 2 * EPOCH_DEPTH), jnp.bfloat16),
            jax.ShapeDtypeStruct((EPOCH_ROWS, arrival.shape[1]), jnp.bfloat16),
        ),
        in_specs=[HBM] * len(taken),
        out_specs=[VMEM] * 3,
        scratch_shapes=[pltpu.VMEM(array.shape, array.dtype) for array in taken]
        + [pltpu.SemaphoreType.DMA((3,)), pltpu.SemaphoreType.DMA((1, 2))],
        compiler_params=pltpu.CompilerParams(vmem_limit_bytes=24 << 20),
        name="pack",
    )(*(pltpu.with_memory_space_constraint(array, pltpu.HBM) for array in taken))


def sweeps_kernel(
    received_ref, design_ref, spread_ref, footprint_ref, cells_ref, phase_ref, quality_ref, parts_ref,
    motion_ref, weighted_ref, modeled_ref,
):
    pairs, pixels = phase_ref.shape
    chunks = pixels // LANES
    swap = swap_rows(SUBLANES, scale_squared)
    for group in range(0, pairs // GROUP, 2):
        taken = [received_ref[pl.ds((group + side) * LANES, LANES), :] for side in range(2)]
        swapped = jnp.dot(swap, jnp.concatenate(taken, axis=1), preferred_element_type=jnp.float32)
        for side in range(2):
            lanes = swapped[:, side * LANES : (side + 1) * LANES]
            for c in range(chunks):
                rows, columns = pl.ds((group + side) * GROUP, GROUP), pl.ds(c * LANES, LANES)
                phase = lanes[c * GROUP : (c + 1) * GROUP]
                quality = lanes[(chunks + c) * GROUP : (chunks + c + 1) * GROUP]
                phase_ref[rows, columns] = phase
                quality_ref[rows, columns] = quality
                weighted_ref[rows, columns] = (quality * phase / (scale_squared + phase * phase)).astype(
                    jnp.bfloat16
                )
    parts_ref[...] = jnp.zeros_like(parts_ref)
    for repeat in range(ITERS):
        for half in range(0, pixels, HALF):
            columns = pl.ds(half, HALF)
            if repeat > 0:
                for k in range(0, pairs, LANES):
                    rows = pl.ds(k, LANES)
                    residual = phase_ref[rows, columns] - modeled_ref[rows, columns]
                    weighted_ref[rows, columns] = (
                        quality_ref[rows, columns] * residual / (scale_squared + residual * residual)
                    ).astype(jnp.bfloat16)
            motion = jnp.dot(spread_ref[...], weighted_ref[:, columns], preferred_element_type=jnp.float32)
            if repeat > 0:
                motion = motion_ref[:, columns] + motion
            motion_ref[:, columns] = motion
            high = motion.astype(jnp.bfloat16)
            parts_ref[0:EPOCH_ROWS, columns] = high
            parts_ref[EPOCH_DEPTH : EPOCH_DEPTH + EPOCH_ROWS, columns] = (
                motion - high.astype(jnp.float32)
            ).astype(jnp.bfloat16)
            if repeat < ITERS - 1:
                modeled_ref[:, columns] = jnp.dot(
                    design_ref[...], parts_ref[:, columns], preferred_element_type=jnp.float32
                )
    targets = lax.broadcasted_iota(jnp.int32, (SUBLANES, pixels), 0)
    onehot = (targets == footprint_ref[...]).astype(jnp.bfloat16)
    cells_ref[...] = lax.dot_general(
        onehot, parts_ref[0:EPOCH_DEPTH, :], (((1,), (1,)), ((), ())), preferred_element_type=jnp.float32
    )


def sweeps(received, design, spread, footprint):
    pairs = design.shape[0]
    pixels = footprint.shape[1]
    return pl.pallas_call(
        sweeps_kernel,
        out_shape=(
            jax.ShapeDtypeStruct((SUBLANES, EPOCH_DEPTH), jnp.float32),
            jax.ShapeDtypeStruct((pairs, pixels), jnp.float32),
            jax.ShapeDtypeStruct((pairs, pixels), jnp.float32),
            jax.ShapeDtypeStruct((2 * EPOCH_DEPTH, pixels), jnp.bfloat16),
        ),
        in_specs=[VMEM] * 4,
        out_specs=[VMEM] * 4,
        scratch_shapes=[
            pltpu.VMEM((EPOCH_ROWS, pixels), jnp.float32),
            pltpu.VMEM((pairs, pixels), jnp.bfloat16),
            pltpu.VMEM((pairs, pixels), jnp.float32),
        ],
        compiler_params=pltpu.CompilerParams(vmem_limit_bytes=24 << 20),
        name="sweeps",
    )(received, design, spread, footprint)


def misfit_kernel(design_ref, phase_ref, quality_ref, parts_ref, misfit_ref, modeled_ref):
    pairs, pixels = phase_ref.shape
    for half in range(0, pixels, HALF):
        columns = pl.ds(half, HALF)
        modeled_ref[:, columns] = jnp.dot(
            design_ref[...], parts_ref[:, columns], preferred_element_type=jnp.float32
        )
    for half in range(0, pixels, HALF):
        columns = pl.ds(half, HALF)
        above = jnp.zeros((SUBLANES, HALF), jnp.float32)
        below = jnp.zeros((SUBLANES, HALF), jnp.float32)
        for k in range(0, pairs, SUBLANES):
            rows = pl.ds(k, SUBLANES)
            residual = phase_ref[rows, columns] - modeled_ref[rows, columns]
            square = residual * residual
            weight = quality_ref[rows, columns] / (scale_squared + square)
            above += weight * square
            below += weight
        misfit_ref[:, columns] = jnp.sum(above, axis=0, keepdims=True) / jnp.sum(below, axis=0, keepdims=True)


def misfits(design, phase, quality, parts):
    pairs, pixels = phase.shape
    return pl.pallas_call(
        misfit_kernel,
        out_shape=jax.ShapeDtypeStruct((1, pixels), jnp.float32),
        in_specs=[VMEM] * 4,
        out_specs=VMEM,
        scratch_shapes=[pltpu.VMEM((pairs, pixels), jnp.float32)],
        compiler_params=pltpu.CompilerParams(vmem_limit_bytes=24 << 20),
        name="misfit",
    )(design, phase, quality, parts)


def body(interferograms, coherence, pair_epochs, inverse, footprint):
    devices = lax.axis_size("pair")
    order = exchange_order(devices)
    packed, design, spread = pack(interferograms, coherence, pair_epochs, inverse, order)
    blocks = lax.all_to_all(
        packed.reshape(devices, packed.shape[0] // devices, LANES),
        "pair",
        split_axis=0,
        concat_axis=0,
        tiled=True,
        axis_index_groups=[order],
    )
    cells, phase, quality, parts = sweeps(blocks.reshape(packed.shape), design, spread, footprint)
    cells_tile = footprint.shape[1] // PPC
    epochs = inverse.shape[0]
    own_cells = cells[:cells_tile, :epochs]
    spilled = cells[cells_tile : 2 * cells_tile, :epochs]
    arrived = from_behind(spilled, ("pair", "col"), 1)
    misfit = misfits(design, phase, quality, parts)
    return (misfit, (own_cells + arrived).T)


def solution(mesh):
    in_specs = (P("pair", None, "col"), P("pair", None, "col"), P(), P(), P("pair", "col"))
    out_specs = (P("pair", "col"), P(None, ("pair", "col")))
    return jax.shard_map(body, mesh=mesh, in_specs=in_specs, out_specs=out_specs, check_vma=False)
```

```python
import jax
import jax.numpy as jnp
import numpy as np
from jax import lax
from jax.experimental import pallas as pl
from jax.experimental.pallas import tpu as pltpu
from jax.sharding import PartitionSpec as P

PPC = 256
ITERS = 4
LANES = 128
SUBLANES = 8
GROUP = 16
EPOCH_ROWS = 160
EPOCH_DEPTH = 256
HALF = 256
ORDER_SEED = 121

phase_scale = 1.5
scale_squared = phase_scale**2

VMEM = pl.BlockSpec(memory_space=pltpu.VMEM)
HBM = pl.BlockSpec(memory_space=pltpu.HBM)


def exchange_order(devices):
    halves = np.random.RandomState(ORDER_SEED).permutation(devices // 2)
    return [int(2 * half + side) for half in halves for side in range(2)]


def from_behind(block, axis, distance):
    devices = range(lax.axis_size(axis))
    route = [(i - distance, i) for i in devices if i - distance in devices]
    return lax.ppermute(block, axis, route)


def swap_rows(outer, scale_late):
    inner = LANES // outer
    row = lax.broadcasted_iota(jnp.int32, (LANES, LANES), 0)
    column = lax.broadcasted_iota(jnp.int32, (LANES, LANES), 1)
    hit = (row // inner == column % outer) & (row % inner == column // outer)
    value = jnp.where(row >= LANES // 2, scale_late, 1.0)
    return jnp.where(hit, value, 0.0).astype(jnp.bfloat16)


def reorder_pairs(arrival_ref, named_ref, design_ref, reorder_ref):
    pairs = named_ref.shape[1]
    reorder = (lax.broadcasted_iota(jnp.int32, (pairs, pairs), 0) == arrival_ref[...]).astype(jnp.bfloat16)
    named = jnp.dot(
        named_ref[...].astype(jnp.float32).astype(jnp.bfloat16), reorder, preferred_element_type=jnp.float32
    )
    epochs = lax.broadcasted_iota(jnp.int32, (EPOCH_DEPTH, pairs), 0).astype(jnp.float32)
    later = (epochs == named[1:2, :]).astype(jnp.float32)
    earlier = (epochs == named[0:1, :]).astype(jnp.float32)
    design = (later - earlier).T.astype(jnp.bfloat16)
    design_ref[:, 0:EPOCH_DEPTH] = design
    design_ref[:, EPOCH_DEPTH:] = design
    reorder_ref[...] = reorder


def pack_kernel(
    order, phase_hbm, quality_hbm, arrival_hbm, named_hbm, packed_ref, design_ref, reorder_ref,
    phase_ref, quality_ref, arrival_ref, named_ref, small_sems, sems,
):
    pairs, slabs, pixels = phase_ref.shape
    step = slabs // sems.shape[0]
    small = [
        pltpu.make_async_copy(source, target, small_sems.at[at])
        for at, (source, target) in enumerate(
            ((arrival_hbm, arrival_ref), (named_hbm, named_ref))
        )
    ]
    large = []
    for part in range(sems.shape[0]):
        for which, (source, target) in enumerate(((phase_hbm, phase_ref), (quality_hbm, quality_ref))):
            span = pl.ds(part * step, step)
            large.append(
                pltpu.make_async_copy(source.at[:, span, :], target.at[:, span, :], sems.at[part, which])
            )
    for copy in small + large:
        copy.start()
    for copy in small:
        copy.wait()
    reorder_pairs(arrival_ref, named_ref, design_ref, reorder_ref)
    place = {slab: at for at, slab in enumerate(order)}
    swap = swap_rows(GROUP, 1.0)
    for group in range(slabs // GROUP):
        if group * GROUP % step == 0:
            for copy in large[2 * (group * GROUP // step) :][:2]:
                copy.wait()
        rows = [
            jnp.concatenate(
                [ref[k, pl.ds(group * GROUP, GROUP), pl.ds(c * LANES, LANES)] for k in range(pairs)], axis=1
            )
            for ref in (phase_ref, quality_ref)
            for c in range(pixels // LANES)
        ]
        swapped = jnp.dot(swap, jnp.concatenate(rows, axis=0), preferred_element_type=jnp.float32)
        for slab in range(0, GROUP, 2):
            tiles = [
                swapped[s * SUBLANES : (s + 1) * SUBLANES, k * LANES : (k + 1) * LANES]
                for s in (slab, slab + 1)
                for k in range(pairs)
            ]
            first = place[group * GROUP + slab] * pairs * SUBLANES
            for at in range(0, len(tiles), 2):
                packed_ref[pl.ds(first + at * SUBLANES, 2 * SUBLANES), :] = jnp.concatenate(
                    tiles[at : at + 2], axis=0
                ).astype(jnp.bfloat16)


def pack(interferograms, coherence, pair_epochs, order):
    pairs, slabs, pixels = interferograms.shape
    rows = slabs * pairs * 2 * pixels // LANES
    arrival = np.array([[device * pairs + k for device in order for k in range(pairs)]], np.int32)
    taken = (interferograms, coherence, jnp.asarray(arrival), pair_epochs.T)
    return pl.pallas_call(
        lambda *refs: pack_kernel(order, *refs),
        out_shape=(
            jax.ShapeDtypeStruct((rows, LANES), jnp.bfloat16),
            jax.ShapeDtypeStruct((arrival.shape[1], 2 * EPOCH_DEPTH), jnp.bfloat16),
            jax.ShapeDtypeStruct((arrival.shape[1], arrival.shape[1]), jnp.bfloat16),
        ),
        in_specs=[HBM] * len(taken),
        out_specs=[VMEM] * 3,
        scratch_shapes=[pltpu.VMEM(array.shape, array.dtype) for array in taken]
        + [pltpu.SemaphoreType.DMA((2,)), pltpu.SemaphoreType.DMA((1, 2))],
        compiler_params=pltpu.CompilerParams(vmem_limit_bytes=24 << 20),
        name="pack",
    )(*(pltpu.with_memory_space_constraint(array, pltpu.HBM) for array in taken))


def sweeps_kernel(
    received_ref, design_ref, reorder_ref, inverse_ref, footprint_ref, cells_ref, phase_ref, quality_ref, parts_ref,
    spread_ref, motion_ref, weighted_ref, modeled_ref,
):
    pairs, pixels = phase_ref.shape
    chunks = pixels // LANES
    swap = swap_rows(SUBLANES, scale_squared)
    for group in range(0, pairs // GROUP, 2):
        taken = [received_ref[pl.ds((group + side) * LANES, LANES), :] for side in range(2)]
        swapped = jnp.dot(swap, jnp.concatenate(taken, axis=1), preferred_element_type=jnp.float32)
        for side in range(2):
            lanes = swapped[:, side * LANES : (side + 1) * LANES]
            for c in range(chunks):
                rows, columns = pl.ds((group + side) * GROUP, GROUP), pl.ds(c * LANES, LANES)
                phase = lanes[c * GROUP : (c + 1) * GROUP]
                quality = lanes[(chunks + c) * GROUP : (chunks + c + 1) * GROUP]
                phase_ref[rows, columns] = phase
                quality_ref[rows, columns] = quality
                weighted_ref[rows, columns] = (quality * phase / (scale_squared + phase * phase)).astype(
                    jnp.bfloat16
                )
    parts_ref[...] = jnp.zeros_like(parts_ref)
    spread_ref[...] = jnp.zeros_like(spread_ref)
    spread_ref[0 : inverse_ref.shape[0], :] = jnp.dot(
        inverse_ref[...], reorder_ref[...], preferred_element_type=jnp.float32
    ).astype(jnp.bfloat16)
    for repeat in range(ITERS):
        for half in range(0, pixels, HALF):
            columns = pl.ds(half, HALF)
            if repeat > 0:
                for k in range(0, pairs, LANES):
                    rows = pl.ds(k, LANES)
                    residual = phase_ref[rows, columns] - modeled_ref[rows, columns]
                    weighted_ref[rows, columns] = (
                        quality_ref[rows, columns] * residual / (scale_squared + residual * residual)
                    ).astype(jnp.bfloat16)
            motion = jnp.dot(spread_ref[...], weighted_ref[:, columns], preferred_element_type=jnp.float32)
            if repeat > 0:
                motion = motion_ref[:, columns] + motion
            motion_ref[:, columns] = motion
            high = motion.astype(jnp.bfloat16)
            parts_ref[0:EPOCH_ROWS, columns] = high
            parts_ref[EPOCH_DEPTH : EPOCH_DEPTH + EPOCH_ROWS, columns] = (
                motion - high.astype(jnp.float32)
            ).astype(jnp.bfloat16)
            if repeat < ITERS - 1:
                modeled_ref[:, columns] = jnp.dot(
                    design_ref[...], parts_ref[:, columns], preferred_element_type=jnp.float32
                )
    targets = lax.broadcasted_iota(jnp.int32, (SUBLANES, pixels), 0)
    onehot = (targets == footprint_ref[...]).astype(jnp.bfloat16)
    cells_ref[...] = lax.dot_general(
        onehot, parts_ref[0:EPOCH_DEPTH, :], (((1,), (1,)), ((), ())), preferred_element_type=jnp.float32
    )


def sweeps(received, design, reorder, inverse, footprint):
    pairs = design.shape[0]
    pixels = footprint.shape[1]
    return pl.pallas_call(
        sweeps_kernel,
        out_shape=(
            jax.ShapeDtypeStruct((SUBLANES, EPOCH_DEPTH), jnp.float32),
            jax.ShapeDtypeStruct((pairs, pixels), jnp.float32),
            jax.ShapeDtypeStruct((pairs, pixels), jnp.float32),
            jax.ShapeDtypeStruct((2 * EPOCH_DEPTH, pixels), jnp.bfloat16),
        ),
        in_specs=[VMEM] * 5,
        out_specs=[VMEM] * 4,
        scratch_shapes=[
            pltpu.VMEM((EPOCH_ROWS, pairs), jnp.bfloat16),
            pltpu.VMEM((EPOCH_ROWS, pixels), jnp.float32),
            pltpu.VMEM((pairs, pixels), jnp.bfloat16),
            pltpu.VMEM((pairs, pixels), jnp.float32),
        ],
        compiler_params=pltpu.CompilerParams(vmem_limit_bytes=24 << 20),
        name="sweeps",
    )(received, design, reorder, inverse, footprint)


def misfit_kernel(design_ref, phase_ref, quality_ref, parts_ref, misfit_ref, modeled_ref):
    pairs, pixels = phase_ref.shape
    for half in range(0, pixels, HALF):
        columns = pl.ds(half, HALF)
        modeled_ref[:, columns] = jnp.dot(
            design_ref[...], parts_ref[:, columns], preferred_element_type=jnp.float32
        )
    for half in range(0, pixels, HALF):
        columns = pl.ds(half, HALF)
        above = jnp.zeros((SUBLANES, HALF), jnp.float32)
        below = jnp.zeros((SUBLANES, HALF), jnp.float32)
        for k in range(0, pairs, SUBLANES):
            rows = pl.ds(k, SUBLANES)
            residual = phase_ref[rows, columns] - modeled_ref[rows, columns]
            square = residual * residual
            weight = quality_ref[rows, columns] / (scale_squared + square)
            above += weight * square
            below += weight
        misfit_ref[:, columns] = jnp.sum(above, axis=0, keepdims=True) / jnp.sum(below, axis=0, keepdims=True)


def misfits(design, phase, quality, parts):
    pairs, pixels = phase.shape
    return pl.pallas_call(
        misfit_kernel,
        out_shape=jax.ShapeDtypeStruct((1, pixels), jnp.float32),
        in_specs=[VMEM] * 4,
        out_specs=VMEM,
        scratch_shapes=[pltpu.VMEM((pairs, pixels), jnp.float32)],
        compiler_params=pltpu.CompilerParams(vmem_limit_bytes=24 << 20),
        name="misfit",
    )(design, phase, quality, parts)


def body(interferograms, coherence, pair_epochs, inverse, footprint):
    devices = lax.axis_size("pair")
    order = exchange_order(devices)
    packed, design, reorder = pack(interferograms, coherence, pair_epochs, order)
    blocks = lax.all_to_all(
        packed.reshape(devices, packed.shape[0] // devices, LANES),
        "pair",
        split_axis=0,
        concat_axis=0,
        tiled=True,
        axis_index_groups=[order],
    )
    cells, phase, quality, parts = sweeps(blocks.reshape(packed.shape), design, reorder, inverse, footprint)
    cells_tile = footprint.shape[1] // PPC
    epochs = inverse.shape[0]
    own_cells = cells[:cells_tile, :epochs]
    spilled = cells[cells_tile : 2 * cells_tile, :epochs]
    arrived = from_behind(spilled, ("pair", "col"), 1)
    misfit = misfits(design, phase, quality, parts)
    return (misfit, (own_cells + arrived).T)


def solution(mesh):
    in_specs = (P("pair", None, "col"), P("pair", None, "col"), P(), P(), P("pair", "col"))
    out_specs = (P("pair", "col"), P(None, ("pair", "col")))
    return jax.shard_map(body, mesh=mesh, in_specs=in_specs, out_specs=out_specs, check_vma=False)
```
